32 devices in a mesh: dom: 16 (over z, y, core), sub: 2 (over x).
Axes of the slice: x: 2, y: 2, z: 4, core: 2. Of those that a mesh axis runs over, the one named last changes fastest.
Arguments:
- rhs: float32 [2, 24576], P(None, ('dom', 'sub')), may hold values from -6 to 6
- start: float32 [2, 24576], P(None, ('dom', 'sub')), may hold values from -6 to 6
- stiffness: bfloat16 [24576, 768], P(('dom', 'sub')), may hold values from -0.109375 to 0.109375
- local_inverse: bfloat16 [24576, 768], P(('dom', 'sub')), may hold values from -0.109375 to 0.109375
- basis: bfloat16 [24, 24576], P(None, ('dom', 'sub')), may hold values from -0.21875 to 0.21875
- weights: float32 [24576], P(('dom', 'sub')), may hold values from 0.3 to 1
- coarse_inverse: float32 [768, 768], P(('dom', 'sub')), may hold values from -0.4375 to 0.4375
- orders: int32 [32], P(('dom', 'sub')), may hold values from 192 to 768, as said below
- out_rows: int32 [32, 6, 128], P(('dom', 'sub')), may hold values from 0 to 191
- out_counts: int32 [32, 6], P(('dom', 'sub')), may hold values from 0 to 128, as said below
- in_rows: int32 [32, 6, 128], P(('dom', 'sub')), may hold values from 0 to 191
Outputs:
- solution: float32 [2, 24576], P(None, ('dom', 'sub'))
- residual: float32 [2, 24576], P(None, ('dom', 'sub'))
The draws below stay inside these ranges and needn't reach their ends.
Inputs may be any that keep to these rules, and one draw needn't show every extreme that they name: `orders`: some subdomain has order exactly 768, another exactly 192. `out_rows`: every listed row lies below every subdomain's order. `in_rows`: every listed row lies below every subdomain's order. `out_counts`: some direction of some subdomain uses all 128 slots.
All inputs are finite; a program needn't handle non-finite values.
Results may differ from the reference program's by a relative error of at most 0.0019.
Values sent between devices are 32-bit elements; how exact they have to be, the bound alone decides.
A program may use at most 64 MiB of HBM per device.

```python
import jax
import jax.numpy as jnp
from jax import lax

SUB_N = 768
NV = 24
H = 128
LOADS = 2
ITERS = 1
DOMAINS = 32
ROWS = 24576
NC = 768
N_DOM = 16
N_SUB = 2


def draw_orders(key, part):
    orders_drawn = jax.random.randint(key, (DOMAINS,), SUB_N // 4, SUB_N + 1)
    chosen = jax.random.randint(jax.random.fold_in(key, 7), (), 0, DOMAINS)
    orders_drawn = orders_drawn.at[chosen].set(SUB_N)
    orders_drawn = orders_drawn.at[(chosen + 1) % DOMAINS].set(SUB_N // 4)
    return orders_drawn.astype(jnp.int32)


def draw_out_counts(key, part):
    counts_drawn = jax.random.randint(key, (DOMAINS, 6), 0, H + 1)
    chosen = jax.random.randint(jax.random.fold_in(key, 11), (), 0, DOMAINS)
    counts_drawn = counts_drawn.at[chosen, 0].set(H)
    return counts_drawn.astype(jnp.int32)


def touch_ends(result, own_key, least, top_value):
    longest = result.shape.index(max(result.shape))
    spots = []
    for shift in (0, 1):
        where = [jax.random.randint(jax.random.fold_in(own_key, axis), (), 0, length) for axis, length in enumerate(result.shape)]
        where[longest] = (where[longest] + shift) % result.shape[longest]
        spots.append(tuple(where))
    return result.at[spots[0]].set(least).at[spots[1]].set(top_value)


def raised(values, own_key, source, target, shards_of, factor):
    def block_of(dim):
        return (jnp.arange(values.shape[dim]) // (values.shape[dim] // shards_of)).reshape((-1,) + (1,) * (values.ndim - 1 - dim))

    near = jax.random.permutation(own_key, shards_of)[block_of(target)]
    other_side = (block_of(target) + shards_of // 2) % shards_of
    return jnp.where((block_of(source) == near) | (block_of(source) == other_side), factor * values, values)


def steps_of(stream_key, extent, shards, low, top_value):
    gain, own = 1.0, jax.random.fold_in(stream_key, 6)
    for dim, blocks in shards:
        heights = jnp.exp(jax.random.uniform(jax.random.fold_in(own, dim), (blocks,), jnp.float32, low / len(shards), top_value / len(shards)))
        gain = gain * jnp.repeat(heights, extent[dim] // blocks).reshape([-1 if axis == dim else 1 for axis in range(len(extent))])
    return gain


def centred(stream_key, shape, width, limit, split=(), dtype=jnp.bfloat16):
    drawn = jax.random.normal(stream_key, shape, jnp.float32) * width
    if len(split) > 0:
        drawn = steps_of(stream_key, shape, split, -0.22, 0.18) * drawn
    return jnp.clip(drawn, min=-limit, max=limit).astype(dtype)


def noise_with(rng, dims, deviation, bound, pieces, heavy, dtype=jnp.bfloat16):
    array = deviation * jax.random.normal(rng, dims, jnp.float32)
    if pieces:
        array = array * steps_of(rng, dims, pieces, -0.22, 0.18)
    return jnp.clip(raised(array, jax.random.fold_in(rng, 3), *heavy), -bound, bound).astype(dtype)


def setup_inputs(seed: int = 0) -> dict:
    key_of = jax.random.split(jax.random.key(seed), 12)
    return {
        "rhs": centred(key_of[0], (LOADS, ROWS), 1.0, 6.0, ((1, 32),), jnp.float32),
        "start": centred(key_of[1], (LOADS, ROWS), 1.0, 6.0, ((1, 32),), jnp.float32),
        "stiffness": centred(key_of[2], (ROWS, SUB_N), (4 * SUB_N) ** -0.5, 0.109375, ((0, 32),)),
        "local_inverse": centred(key_of[3], (ROWS, SUB_N), (4 * SUB_N) ** -0.5, 0.109375, ((0, 32),)),
        "basis": centred(key_of[4], (NV, ROWS), SUB_N ** -0.5, 0.21875, ((1, 32),)),
        "weights": jnp.clip(0.3 + 0.7 * jax.random.uniform(key_of[5], (ROWS,), jnp.float32) ** steps_of(key_of[5], (ROWS,), ((0, 32),), -0.2, 0.2), 0.3, 1.0),
        "coarse_inverse": noise_with(key_of[6], (NC, NC), NC ** -0.5, 0.4375, ((0, 32),), (1, 0, 32, 2.75), jnp.float32),
        "orders": draw_orders(jax.random.fold_in(key_of[11], 71), 0),
        "out_rows": touch_ends(jax.random.randint(key_of[8], (DOMAINS, 6, H), 0, SUB_N // 4), jax.random.fold_in(key_of[8], 1), 0, (SUB_N // 4) - 1).astype(jnp.int32),
        "out_counts": draw_out_counts(jax.random.fold_in(key_of[11], 71), 0),
        "in_rows": touch_ends(jax.random.randint(key_of[10], (DOMAINS, 6, H), 0, SUB_N // 4), jax.random.fold_in(key_of[10], 1), 0, (SUB_N // 4) - 1).astype(jnp.int32),
    }


DIRECTIONS = (("sub", 1), ("sub", -1), ("dom", 1), ("dom", -1), ("dom", 2), ("dom", -2))


def shifted(grid, axis_pos, offset):
    moved = jnp.roll(grid, offset, axis=axis_pos)
    length = grid.shape[axis_pos]
    where_from = jnp.arange(length) - offset
    valid = (where_from >= 0) & (where_from < length)
    if axis_pos == 0:
        valid = valid[:, None, None, None]
    else:
        valid = valid[None, :, None, None]
    return jnp.where(valid, moved, jnp.zeros_like(moved))


def add_rows(summed, rows_here, arrived):
    return summed.at[:, rows_here].add(arrived)


def assemble(terms, out_rows, out_counts, in_rows):
    slot_ids = jnp.arange(H)
    summed = terms
    for index_dir, (axis_name, offset) in enumerate(DIRECTIONS):
        index_rows = jnp.broadcast_to(out_rows[:, index_dir, :][:, None, :], (DOMAINS, LOADS, H))
        picked = jnp.take_along_axis(terms, index_rows, axis=2)
        used = (slot_ids[None, None, :] < out_counts[:, index_dir][:, None, None]).astype(jnp.float32)
        picked = picked * used
        grid = picked.reshape(N_DOM, N_SUB, LOADS, H)
        axis_pos = 0 if axis_name == "dom" else 1
        arrived = shifted(grid, axis_pos, offset).reshape(DOMAINS, LOADS, H)
        summed = jax.vmap(add_rows)(summed, in_rows[:, index_dir, :], arrived)
    return summed


def per_domain(field):
    return field.reshape(LOADS, DOMAINS, SUB_N).transpose(1, 0, 2)


def batch_dot(pair):
    return jnp.dot(pair[0], pair[1], preferred_element_type=jnp.float32)


def batch_dot_right(pair):
    return jnp.dot(pair[0], pair[1].T, preferred_element_type=jnp.float32)


def reference(rhs, start, stiffness, local_inverse, basis, weights, coarse_inverse, orders, out_rows, out_counts, in_rows):
    row_mask = (jnp.arange(SUB_N)[None, :] < orders[:, None]).astype(jnp.float32)[:, None, :]
    loads_rhs = per_domain(rhs)
    iterate = per_domain(start) * row_mask
    stiff_blocks = stiffness.reshape(DOMAINS, SUB_N, SUB_N)
    inverse_blocks = local_inverse.reshape(DOMAINS, SUB_N, SUB_N)
    basis_blocks = basis.reshape(NV, DOMAINS, SUB_N).transpose(1, 0, 2)
    weight_rows = weights.reshape(DOMAINS, 1, SUB_N)
    residual = loads_rhs
    for step in range(ITERS):
        iterate_bf = iterate.astype(jnp.bfloat16)
        product = lax.map(batch_dot, (iterate_bf, stiff_blocks))
        residual = row_mask * (loads_rhs - assemble(product, out_rows, out_counts, in_rows))
        residual_bf = residual.astype(jnp.bfloat16)
        local_fix = lax.map(batch_dot, (residual_bf, inverse_blocks))
        coarse_in = lax.map(batch_dot_right, (residual_bf, basis_blocks))
        coarse_all = coarse_in.transpose(1, 0, 2).reshape(LOADS, NC)
        coarse_out = lax.dot_general(coarse_all, coarse_inverse, (((1,), (1,)), ((), ())), precision=lax.Precision.HIGHEST, preferred_element_type=jnp.float32)
        coarse_bf = coarse_out.reshape(LOADS, DOMAINS, NV).transpose(1, 0, 2).astype(jnp.bfloat16)
        coarse_fix = lax.map(batch_dot, (coarse_bf, basis_blocks))
        correction = weight_rows * row_mask * (local_fix + coarse_fix)
        iterate = iterate + assemble(correction, out_rows, out_counts, in_rows)
    solution = iterate.transpose(1, 0, 2).reshape(LOADS, ROWS)
    residual_out = residual.transpose(1, 0, 2).reshape(LOADS, ROWS)
    return solution, residual_out
```

```python
import functools
import math

import jax
import jax.numpy as jnp
from jax import lax
from jax.experimental import pallas as pl
from jax.experimental.pallas import tpu as pltpu
from jax.sharding import PartitionSpec as P

DIRECTIONS = (("sub", 1), ("sub", -1), ("dom", 1), ("dom", -1), ("dom", 2), ("dom", -2))
MESH = pl.DeviceIdType.MESH
LANES = 128


def halves(x):
    high = x.astype(jnp.bfloat16).astype(jnp.float32)
    return jnp.concatenate([high, x - high], axis=0).astype(jnp.bfloat16)


def dot(a, b):
    return jnp.dot(a, b, preferred_element_type=jnp.float32)


def dot_t(a, b):
    return lax.dot_general(a, b, (((1,), (1,)), ((), ())), preferred_element_type=jnp.float32)


def exact_dot(x, picker, by=dot):
    rows = x.shape[0]
    both = by(halves(x), picker)
    return both[:rows] + both[rows:]


def kernel(
    n_dom,
    n_sub,
    rhs_hbm,
    start_hbm,
    stiff_hbm,
    inverse_hbm,
    basis_hbm,
    weights_hbm,
    coarse_hbm,
    orders_hbm,
    out_rows_hbm,
    out_counts_hbm,
    in_rows_hbm,
    solution_hbm,
    residual_hbm,
    rhs,
    start,
    stiff,
    inverse,
    basis,
    weights,
    coarse,
    orders,
    out_rows,
    out_counts,
    in_rows,
    picker,
    placer,
    basis_pad,
    coarse_pad,
    sent_first,
    sent_second,
    came_first,
    came_second,
    gathered,
    solution_out,
    residual_out,
    load_sems,
    store_sems,
    send_first,
    recv_first,
    send_second,
    recv_second,
    gather_send,
    gather_recv,
):
    devices = n_dom * n_sub
    loads, order_pad = rhs.shape
    slots = out_rows.shape[1]
    vectors = basis.shape[0]
    head = placer.shape[0]
    dom, sub = lax.axis_index("dom"), lax.axis_index("sub")
    me = dom * n_sub + sub

    def load(index, source, target):
        copy = pltpu.make_async_copy(source, target, load_sems.at[index])
        copy.start()
        return copy

    got_start = load(0, start_hbm, start)
    got_orders = load(1, orders_hbm, orders)
    got_head = load(2, stiff_hbm.at[:, :head], stiff.at[:, :head])
    got_out = load(3, out_rows_hbm, out_rows)
    got_counts = load(4, out_counts_hbm, out_counts)
    got_tail = load(5, stiff_hbm.at[:, head:], stiff.at[:, head:])
    got_in = load(6, in_rows_hbm, in_rows)
    got_rhs = load(7, rhs_hbm, rhs)
    got_basis = load(8, basis_hbm, basis)
    got_weights = load(9, weights_hbm, weights)
    got_inverse = load(10, inverse_hbm, inverse)
    got_coarse = load(11, coarse_hbm, coarse)

    came_first[...] = jnp.zeros_like(came_first)
    came_second[...] = jnp.zeros_like(came_second)

    barrier = pltpu.get_barrier_semaphore()

    def device_of(step):
        peer = lax.rem(me + step, devices)
        return (lax.div(peer, n_sub), lax.rem(peer, n_sub))

    def greet(step, carry):
        pl.semaphore_signal(barrier, inc=1, device_id=device_of(step), device_id_type=MESH)
        return carry

    lax.fori_loop(1, devices, greet, 0)

    def exchange(sent, came, send_sems, recv_sems):
        moves = []
        for index_dir, (axis_name, offset) in enumerate(DIRECTIONS):
            here, length = (sub, n_sub) if axis_name == "sub" else (dom, n_dom)
            there = here + offset
            target = (dom, there) if axis_name == "sub" else (there, sub)
            sends = (there >= 0) & (there < length)
            receives = (here - offset >= 0) & (here - offset < length)
            copy = pltpu.make_async_remote_copy(
                src_ref=sent.at[index_dir],
                dst_ref=came.at[index_dir],
                send_sem=send_sems.at[index_dir],
                recv_sem=recv_sems.at[index_dir],
                device_id=target,
                device_id_type=MESH,
            )
            pl.when(sends)(copy.start)
            moves.append((copy, sends, receives))
        return moves

    def wait_arrivals(moves):
        for copy, _, receives in moves:
            pl.when(receives)(copy.wait_recv)

    def arrived_rows(came):
        slot_terms = jnp.concatenate([came[j] for j in range(len(DIRECTIONS))], axis=1)
        return exact_dot(slot_terms, placer[...], dot_t)

    row_ids = lax.broadcasted_iota(jnp.int32, (head, slots), 0)
    slot_ids = lax.broadcasted_iota(jnp.int32, (1, slots), 1)
    got_out.wait()
    got_counts.wait()
    for j in range(len(DIRECTIONS)):
        wanted = jnp.where(slot_ids < out_counts[:, j : j + 1], out_rows[j : j + 1, :], -1)
        picker[:, j * slots : (j + 1) * slots] = (row_ids == wanted).astype(jnp.bfloat16)
    got_start.wait()
    got_orders.wait()
    column_ids = lax.broadcasted_iota(jnp.int32, (1, order_pad), 1)
    row_mask = (column_ids < orders[...]).astype(jnp.float32)
    iterate = start[...] * row_mask
    iterate_bf = iterate.astype(jnp.bfloat16)
    got_head.wait()
    product_head = dot(iterate_bf, stiff[:, :head])
    picked = exact_dot(product_head, picker[...])
    for j in range(len(DIRECTIONS)):
        sent_first[j] = picked[:, j * slots : (j + 1) * slots]
    pl.semaphore_wait(barrier, devices - 1)
    moves_first = exchange(sent_first, came_first, send_first, recv_first)

    got_in.wait()
    for j in range(len(DIRECTIONS)):
        placer[:, j * slots : (j + 1) * slots] = (row_ids == in_rows[j : j + 1, :]).astype(jnp.bfloat16)
    got_rhs.wait()
    got_tail.wait()
    residual_tail = row_mask[:, head:] * (rhs[:, head:] - dot(iterate_bf, stiff[:, head:]))
    residual_out[:, head:] = residual_tail
    tail_bf = residual_tail.astype(jnp.bfloat16)
    got_basis.wait()
    basis_pad[...] = jnp.zeros_like(basis_pad)
    basis_pad[:vectors, :] = basis[...]
    coarse_tail = dot_t(tail_bf, basis_pad[:, head:])
    got_inverse.wait()
    fix_tail = dot(tail_bf, inverse[head:, :])
    got_weights.wait()
    scale = weights[...] * row_mask
    scaled_basis = scale * basis[...].astype(jnp.float32)
    picked_basis = exact_dot(scaled_basis[:, :head], picker[...])

    got_coarse.wait()
    group = math.lcm(vectors, LANES) // vectors
    lane_ids = lax.broadcasted_iota(jnp.int32, (vectors, LANES), 1)

    def spread(block, carry):
        base = pl.multiple_of(block * group * vectors, LANES)
        tiles = [
            coarse[:, pl.ds(base + t * LANES, LANES)] for t in range(group * vectors // LANES)
        ]
        for r in range(group):
            tile, first = divmod(r * vectors, LANES)
            moved = pltpu.roll(tiles[tile], LANES - first, 1) if first else tiles[tile]
            if first + vectors > LANES:
                following = pltpu.roll(tiles[tile + 1], LANES - first, 1)
                moved = jnp.where(lane_ids < LANES - first, moved, following)
            coarse_pad[block * group + r] = jnp.where(lane_ids < vectors, moved, 0.0)
        return carry

    lax.fori_loop(0, devices // group, spread, 0)

    wait_arrivals(moves_first)
    residual_head = row_mask[:, :head] * (rhs[:, :head] - (product_head + arrived_rows(came_first)))
    head_bf = residual_head.astype(jnp.bfloat16)
    gathered[me] = coarse_tail + dot_t(head_bf, basis_pad[:, :head])

    def send_coarse(step):
        return pltpu.make_async_remote_copy(
            src_ref=gathered.at[me],
            dst_ref=gathered.at[me],
            send_sem=gather_send,
            recv_sem=gather_recv,
            device_id=device_of(step),
            device_id_type=MESH,
        )

    def start_coarse(step, carry):
        send_coarse(step).start()
        return carry

    lax.fori_loop(1, devices, start_coarse, 0)

    residual_out[:, :head] = residual_head
    put_residual = pltpu.make_async_copy(residual_out, residual_hbm, store_sems.at[0])
    put_residual.start()
    fixed = scale * (fix_tail + dot(head_bf, inverse[:head, :]))
    picked_fix = exact_dot(fixed[:, :head], picker[...])
    base_out = iterate + fixed

    others = gathered.at[pl.ds(0, devices - 1)]
    pltpu.make_async_copy(others, others, gather_recv).wait()

    def accumulate(block, sums):
        sums = list(sums)
        for r in range(group):
            d = block * group + r
            terms, rows = gathered[d], coarse_pad[d]
            for l in range(loads):
                sums[l] = sums[l] + terms[l : l + 1, :] * rows
        return tuple(sums)

    sums = tuple(jnp.zeros((vectors, LANES), jnp.float32) for _ in range(loads))
    if devices // group <= 4:
        for block in range(devices // group):
            sums = accumulate(block, sums)
    else:
        sums = lax.fori_loop(0, devices // group, accumulate, sums)
    coarse_columns = [
        jnp.sum(s, axis=1, keepdims=True).astype(jnp.bfloat16).astype(jnp.float32) for s in sums
    ]

    def spanned(block):
        return jnp.concatenate(
            [jnp.sum(c * block, axis=0, keepdims=True) for c in coarse_columns], axis=0
        )

    picked = picked_fix + spanned(picked_basis)
    for j in range(len(DIRECTIONS)):
        sent_second[j] = picked[:, j * slots : (j + 1) * slots]
    moves_second = exchange(sent_second, came_second, send_second, recv_second)

    base_out = base_out + spanned(scaled_basis)
    solution_out[:, head:] = base_out[:, head:]
    wait_arrivals(moves_second)
    solution_out[:, :head] = base_out[:, :head] + arrived_rows(came_second)
    put_solution = pltpu.make_async_copy(solution_out, solution_hbm, store_sems.at[1])
    put_solution.start()

    for copy, sends, _ in moves_first + moves_second:
        pl.when(sends)(copy.wait_send)
    pltpu.make_async_copy(others, others, gather_send).wait()
    put_residual.wait()
    put_solution.wait()


def per_device(
    n_dom,
    n_sub,
    rhs,
    start,
    stiffness,
    local_inverse,
    basis,
    weights,
    coarse_inverse,
    orders,
    out_rows,
    out_counts,
    in_rows,
):
    loads, order_pad = rhs.shape
    directions, slots = out_rows.shape[1:]
    vectors = basis.shape[0]
    devices = n_dom * n_sub
    head = -(-(order_pad // 4) // LANES) * LANES
    operands = (
        rhs,
        start,
        stiffness,
        local_inverse,
        basis,
        weights.reshape(1, order_pad),
        coarse_inverse,
        orders.reshape(1, 1),
        out_rows.reshape(directions, slots),
        out_counts,
        in_rows.reshape(directions, slots),
    )
    f32 = jnp.float32
    shared = pltpu.VMEM((directions, loads, slots), f32)
    dma = pltpu.SemaphoreType.DMA
    any_space = pl.BlockSpec(memory_space=pl.ANY)
    field = jax.ShapeDtypeStruct((loads, order_pad), f32)
    return pl.pallas_call(
        functools.partial(kernel, n_dom, n_sub),
        out_shape=(field, field),
        in_specs=[any_space] * len(operands),
        out_specs=(any_space, any_space),
        scratch_shapes=[pltpu.VMEM(x.shape, x.dtype) for x in operands]
        + [
            pltpu.VMEM((head, directions * slots), jnp.bfloat16),
            pltpu.VMEM((head, directions * slots), jnp.bfloat16),
            pltpu.VMEM((LANES, order_pad), jnp.bfloat16),
            pltpu.VMEM((devices, vectors, LANES), f32),
            shared,
            shared,
            shared,
            shared,
            pltpu.VMEM((devices, loads, LANES), f32),
            pltpu.VMEM((loads, order_pad), f32),
            pltpu.VMEM((loads, order_pad), f32),
            dma((12,)),
            dma((2,)),
            dma((directions,)),
            dma((directions,)),
            dma((directions,)),
            dma((directions,)),
            dma,
            dma,
        ],
        compiler_params=pltpu.CompilerParams(
            collective_id=0, has_side_effects=True, vmem_limit_bytes=40 * 1024 * 1024
        ),
    )(*operands)


def solution(mesh):
    return jax.shard_map(
        functools.partial(per_device, mesh.shape["dom"], mesh.shape["sub"]),
        mesh=mesh,
        in_specs=(
            P(None, ("dom", "sub")),
            P(None, ("dom", "sub")),
            P(("dom", "sub"), None),
            P(("dom", "sub"), None),
            P(None, ("dom", "sub")),
            P(("dom", "sub")),
            P(("dom", "sub"), None),
            P(("dom", "sub")),
            P(("dom", "sub"), None, None),
            P(("dom", "sub"), None),
            P(("dom", "sub"), None, None),
        ),
        out_specs=(P(None, ("dom", "sub")), P(None, ("dom", "sub"))),
        check_vma=False,
    )
```

```python
import functools
import math

import jax
import jax.numpy as jnp
from jax import lax
from jax.experimental import pallas as pl
from jax.experimental.pallas import tpu as pltpu
from jax.sharding import PartitionSpec as P

DIRECTIONS = (("sub", 1), ("sub", -1), ("dom", 1), ("dom", -1), ("dom", 2), ("dom", -2))
MESH = pl.DeviceIdType.MESH
LANES = 128


def halves(x):
    high = x.astype(jnp.bfloat16).astype(jnp.float32)
    return jnp.concatenate([high, x - high], axis=0).astype(jnp.bfloat16)


def dot(a, b):
    return jnp.dot(a, b, preferred_element_type=jnp.float32)


def dot_t(a, b):
    return lax.dot_general(a, b, (((1,), (1,)), ((), ())), preferred_element_type=jnp.float32)


def exact_dot(x, picker, by=dot):
    rows = x.shape[0]
    both = by(halves(x), picker)
    return both[:rows] + both[rows:]


def kernel(
    n_dom,
    n_sub,
    team,
    rhs_hbm,
    start_hbm,
    stiff_hbm,
    inverse_hbm,
    basis_hbm,
    weights_hbm,
    coarse_hbm,
    orders_hbm,
    out_rows_hbm,
    out_counts_hbm,
    in_rows_hbm,
    solution_hbm,
    residual_hbm,
    rhs,
    start,
    stiff,
    inverse,
    basis,
    weights,
    coarse,
    orders,
    out_rows,
    out_counts,
    in_rows,
    picker,
    placer,
    basis_pad,
    coarse_pad,
    sent_first,
    sent_second,
    came_first,
    came_second,
    gathered,
    solution_out,
    residual_out,
    load_sems,
    store_sems,
    send_first,
    recv_first,
    send_second,
    recv_second,
    team_send,
    team_recv,
    column_send,
    column_recv,
):
    devices = n_dom * n_sub
    loads, order_pad = rhs.shape
    slots = out_rows.shape[2]
    vectors = basis.shape[0]
    head = placer.shape[0]
    dom, sub = lax.axis_index("dom"), lax.axis_index("sub")
    me = dom * n_sub + sub

    def load(index, source, target):
        copy = pltpu.make_async_copy(source, target, load_sems.at[index])
        copy.start()
        return copy

    got_start = load(0, start_hbm, start)
    got_head = load(2, stiff_hbm.at[:, :head], stiff.at[:, :head])
    got_orders = load(1, orders_hbm, orders)
    got_out = load(3, out_rows_hbm, out_rows)
    got_counts = load(4, out_counts_hbm, out_counts)

    came_first[...] = jnp.zeros_like(came_first)
    came_second[...] = jnp.zeros_like(came_second)

    teams = n_dom // team
    place = lax.rem(dom, team)
    team_first = dom - place
    column_id = lax.div(dom, team)

    def wrapped(index, size):
        return jnp.where(index >= size, index - size, index)

    def team_mate(step):
        along, across = divmod(step, n_sub)
        return (team_first + wrapped(place + along, team), wrapped(sub + across, n_sub))

    def column_mate(step):
        return (wrapped(column_id + step, teams) * team + place, sub)

    team_steps, column_steps = range(1, team * n_sub), range(1, teams)
    far = [offset for axis_name, offset in DIRECTIONS if axis_name == "dom"]

    barrier = pltpu.get_barrier_semaphore()

    def greet(device):
        pl.semaphore_signal(barrier, inc=1, device_id=device, device_id_type=MESH)

    greetings = len(team_steps) + len(column_steps)
    for step in column_steps:
        greet(column_mate(step))
    for offset in far:
        inside = (dom + offset >= 0) & (dom + offset < n_dom)
        pl.when(inside)(functools.partial(greet, (dom + offset, sub)))
        greetings = greetings + inside.astype(jnp.int32)
    for step in team_steps:
        greet(team_mate(step))

    got_tail = load(5, stiff_hbm.at[:, head:], stiff.at[:, head:])
    got_in = load(6, in_rows_hbm, in_rows)
    got_rhs = load(7, rhs_hbm, rhs)
    got_basis = load(8, basis_hbm, basis)
    got_inverse = load(10, inverse_hbm, inverse)
    got_weights = load(9, weights_hbm, weights)
    got_coarse = load(11, coarse_hbm, coarse)

    def exchange(sent, came, send_sems, recv_sems):
        moves = []
        for index_dir, (axis_name, offset) in enumerate(DIRECTIONS):
            here, length = (sub, n_sub) if axis_name == "sub" else (dom, n_dom)
            there = here + offset
            target = (dom, there) if axis_name == "sub" else (there, sub)
            sends = (there >= 0) & (there < length)
            receives = (here - offset >= 0) & (here - offset < length)
            copy = pltpu.make_async_remote_copy(
                src_ref=sent.at[index_dir],
                dst_ref=came.at[index_dir],
                send_sem=send_sems.at[index_dir],
                recv_sem=recv_sems.at[index_dir],
                device_id=target,
                device_id_type=MESH,
            )
            pl.when(sends)(copy.start)
            moves.append((copy, sends, receives))
        return moves

    def wait_arrivals(moves):
        for copy, _, receives in moves:
            pl.when(receives)(copy.wait_recv)

    def arrived_rows(came):
        slot_terms = jnp.concatenate([came[j] for j in range(len(DIRECTIONS))], axis=1)
        return exact_dot(slot_terms, placer[...], dot_t)

    row_ids = lax.broadcasted_iota(jnp.int32, (head, slots), 0)
    slot_ids = lax.broadcasted_iota(jnp.int32, (1, slots), 1)
    got_out.wait()
    got_counts.wait()
    for j in range(len(DIRECTIONS)):
        wanted = jnp.where(slot_ids < out_counts[:, j : j + 1], out_rows[j], -1)
        picker[:, j * slots : (j + 1) * slots] = (row_ids == wanted).astype(jnp.bfloat16)
    got_start.wait()
    got_orders.wait()
    column_ids = lax.broadcasted_iota(jnp.int32, (1, order_pad), 1)
    row_mask = (column_ids < orders[...]).astype(jnp.float32)
    iterate = start[...] * row_mask
    iterate_bf = iterate.astype(jnp.bfloat16)
    got_head.wait()
    product_head = dot(iterate_bf, stiff[:, :head])
    picked = exact_dot(product_head, picker[...])
    for j in range(len(DIRECTIONS)):
        sent_first[j] = picked[:, j * slots : (j + 1) * slots]
    pl.semaphore_wait(barrier, greetings)
    moves_first = exchange(sent_first, came_first, send_first, recv_first)

    got_in.wait()
    for j in range(len(DIRECTIONS)):
        placer[:, j * slots : (j + 1) * slots] = (row_ids == in_rows[j]).astype(jnp.bfloat16)
    got_rhs.wait()
    got_tail.wait()
    residual_tail = row_mask[:, head:] * (rhs[:, head:] - dot(iterate_bf, stiff[:, head:]))
    residual_out[:, head:] = residual_tail
    tail_bf = residual_tail.astype(jnp.bfloat16)
    got_basis.wait()
    basis_pad[...] = jnp.zeros_like(basis_pad)
    basis_pad[:vectors, :] = basis[...]
    coarse_tail = dot_t(tail_bf, basis_pad[:, head:])
    got_inverse.wait()
    fix_tail = dot(tail_bf, inverse[head:, :])

    wait_arrivals(moves_first)
    residual_head = row_mask[:, :head] * (rhs[:, :head] - (product_head + arrived_rows(came_first)))
    head_bf = residual_head.astype(jnp.bfloat16)
    gathered[me] = coarse_tail + dot_t(head_bf, basis_pad[:, :head])

    def share(slabs, device, send_sem, recv_sem):
        pltpu.make_async_remote_copy(
            src_ref=gathered.at[slabs],
            dst_ref=gathered.at[slabs],
            send_sem=send_sem,
            recv_sem=recv_sem,
            device_id=device,
            device_id_type=MESH,
        ).start()

    def wait_slabs(count, sem):
        some = gathered.at[pl.ds(0, count)]
        pltpu.make_async_copy(some, some, sem).wait()

    for step in team_steps:
        share(pl.ds(me, 1), team_mate(step), team_send, team_recv)

    residual_out[:, :head] = residual_head
    put_residual = pltpu.make_async_copy(residual_out, residual_hbm, store_sems.at[0])
    put_residual.start()
    got_weights.wait()
    scale = weights[...].reshape(1, order_pad) * row_mask
    fixed = scale * (fix_tail + dot(head_bf, inverse[:head, :]))
    picked_fix = exact_dot(fixed[:, :head], picker[...])
    base_out = iterate + fixed

    mates = team * n_sub
    wait_slabs(mates - 1, team_recv)
    for step in column_steps:
        share(pl.ds(team_first * n_sub, mates), column_mate(step), column_send, column_recv)

    scaled_basis = scale * basis[...].astype(jnp.float32)
    picked_basis = exact_dot(scaled_basis[:, :head], picker[...])

    got_coarse.wait()
    group = math.lcm(vectors, LANES) // vectors
    lane_ids = lax.broadcasted_iota(jnp.int32, (vectors, LANES), 1)

    def spread(block, carry):
        base = pl.multiple_of(block * group * vectors, LANES)
        tiles = [
            coarse[:, pl.ds(base + t * LANES, LANES)] for t in range(group * vectors // LANES)
        ]
        for r in range(group):
            tile, first = divmod(r * vectors, LANES)
            moved = pltpu.roll(tiles[tile], LANES - first, 1) if first else tiles[tile]
            if first + vectors > LANES:
                following = pltpu.roll(tiles[tile + 1], LANES - first, 1)
                moved = jnp.where(lane_ids < LANES - first, moved, following)
            coarse_pad[block * group + r] = jnp.where(lane_ids < vectors, moved, 0.0)
        return carry

    lax.fori_loop(0, devices // group, spread, 0)

    wait_slabs(devices - mates, column_recv)

    def accumulate(block, sums):
        sums = list(sums)
        for r in range(group):
            d = block * group + r
            terms, rows = gathered[d], coarse_pad[d]
            for l in range(loads):
                sums[l] = sums[l] + terms[l : l + 1, :] * rows
        return tuple(sums)

    sums = tuple(jnp.zeros((vectors, LANES), jnp.float32) for _ in range(loads))
    if devices // group <= 4:
        for block in range(devices // group):
            sums = accumulate(block, sums)
    else:
        sums = lax.fori_loop(0, devices // group, accumulate, sums)
    coarse_columns = [
        jnp.sum(s, axis=1, keepdims=True).astype(jnp.bfloat16).astype(jnp.float32) for s in sums
    ]

    def spanned(block):
        return jnp.concatenate(
            [jnp.sum(c * block, axis=0, keepdims=True) for c in coarse_columns], axis=0
        )

    picked = picked_fix + spanned(picked_basis)
    for j in range(len(DIRECTIONS)):
        sent_second[j] = picked[:, j * slots : (j + 1) * slots]
    moves_second = exchange(sent_second, came_second, send_second, recv_second)

    base_out = base_out + spanned(scaled_basis)
    solution_out[:, head:] = base_out[:, head:]
    wait_arrivals(moves_second)
    solution_out[:, :head] = base_out[:, :head] + arrived_rows(came_second)
    put_solution = pltpu.make_async_copy(solution_out, solution_hbm, store_sems.at[1])
    put_solution.start()

    for copy, sends, _ in moves_first + moves_second:
        pl.when(sends)(copy.wait_send)
    wait_slabs(mates - 1, team_send)
    wait_slabs(devices - mates, column_send)
    put_residual.wait()
    put_solution.wait()


def per_device(
    n_dom,
    n_sub,
    rhs,
    start,
    stiffness,
    local_inverse,
    basis,
    weights,
    coarse_inverse,
    orders,
    out_rows,
    out_counts,
    in_rows,
):
    loads, order_pad = rhs.shape
    directions, slots = out_rows.shape[1:]
    team = min(t for t in range(1, n_dom + 1) if n_dom % t == 0 and t * t * n_sub >= n_dom)
    vectors = basis.shape[0]
    devices = n_dom * n_sub
    head = -(-(order_pad // 4) // LANES) * LANES
    operands = (
        rhs,
        start,
        stiffness,
        local_inverse,
        basis,
        weights,
        coarse_inverse,
        orders.reshape(1, 1),
        out_rows.transpose(1, 0, 2),
        out_counts,
        in_rows.transpose(1, 0, 2),
    )
    f32 = jnp.float32
    shared = pltpu.VMEM((directions, loads, slots), f32)
    dma = pltpu.SemaphoreType.DMA
    in_hbm = pl.BlockSpec(memory_space=pltpu.HBM)
    field = jax.ShapeDtypeStruct((loads, order_pad), f32)
    return pl.pallas_call(
        functools.partial(kernel, n_dom, n_sub, team),
        out_shape=(field, field),
        in_specs=[in_hbm] * len(operands),
        out_specs=(in_hbm, in_hbm),
        scratch_shapes=[pltpu.VMEM(x.shape, x.dtype) for x in operands]
        + [
            pltpu.VMEM((head, directions * slots), jnp.bfloat16),
            pltpu.VMEM((head, directions * slots), jnp.bfloat16),
            pltpu.VMEM((LANES, order_pad), jnp.bfloat16),
            pltpu.VMEM((devices, vectors, LANES), f32),
            shared,
            shared,
            shared,
            shared,
            pltpu.VMEM((devices, loads, LANES), f32),
            pltpu.VMEM((loads, order_pad), f32),
            pltpu.VMEM((loads, order_pad), f32),
            dma((12,)),
            dma((2,)),
            dma((directions,)),
            dma((directions,)),
            dma((directions,)),
            dma((directions,)),
            dma,
            dma,
            dma,
            dma,
        ],
        compiler_params=pltpu.CompilerParams(
            collective_id=0, has_side_effects=True, vmem_limit_bytes=63 * 1024 * 1024
        ),
    )(*operands)


def solution(mesh):
    return jax.shard_map(
        functools.partial(per_device, mesh.shape["dom"], mesh.shape["sub"]),
        mesh=mesh,
        in_specs=(
            P(None, ("dom", "sub")),
            P(None, ("dom", "sub")),
            P(("dom", "sub"), None),
            P(("dom", "sub"), None),
            P(None, ("dom", "sub")),
            P(("dom", "sub")),
            P(("dom", "sub"), None),
            P(("dom", "sub")),
            P(("dom", "sub"), None, None),
            P(("dom", "sub"), None),
            P(("dom", "sub"), None, None),
        ),
        out_specs=(P(None, ("dom", "sub")), P(None, ("dom", "sub"))),
        check_vma=False,
    )
```

```python
import functools
import math

import jax
import jax.numpy as jnp
from jax import lax
from jax.experimental import pallas as pl
from jax.experimental.pallas import tpu as pltpu
from jax.sharding import PartitionSpec as P

DIRECTIONS = (("sub", 1), ("sub", -1), ("dom", 1), ("dom", -1), ("dom", 2), ("dom", -2))
MESH = pl.DeviceIdType.MESH
LANES = 128


def halves(x):
    high = x.astype(jnp.bfloat16).astype(jnp.float32)
    return jnp.concatenate([high, x - high], axis=0).astype(jnp.bfloat16)


def dot(a, b):
    return jnp.dot(a, b, preferred_element_type=jnp.float32)


def dot_t(a, b):
    return lax.dot_general(a, b, (((1,), (1,)), ((), ())), preferred_element_type=jnp.float32)


def exact_dot(x, picker, by=dot):
    rows = x.shape[0]
    both = by(halves(x), picker)
    return both[:rows] + both[rows:]


def kernel(
    n_dom,
    n_sub,
    team,
    rhs_hbm,
    start_hbm,
    stiff_hbm,
    inverse_hbm,
    basis_hbm,
    weights_hbm,
    coarse_hbm,
    orders_hbm,
    out_rows_hbm,
    out_counts_hbm,
    in_rows_hbm,
    results_hbm,
    rhs,
    start,
    stiff,
    inverse,
    basis,
    weights,
    coarse,
    orders,
    out_rows,
    out_counts,
    in_rows,
    picker,
    placer,
    basis_pad,
    slot_basis,
    coarse_pad,
    sent_first,
    sent_second,
    came_first,
    came_second,
    gathered,
    results,
    load_sems,
    store_sem,
    send_first,
    recv_first,
    send_second,
    recv_second,
    team_send,
    team_recv,
    column_send,
    column_recv,
):
    devices = n_dom * n_sub
    loads, order_pad = rhs.shape
    slots = out_rows.shape[2]
    vectors = basis.shape[0]
    head = placer.shape[1]
    dom, sub = lax.axis_index("dom"), lax.axis_index("sub")
    me = dom * n_sub + sub

    def load(index, source, target):
        copy = pltpu.make_async_copy(source, target, load_sems.at[index])
        copy.start()
        return copy

    got_start = load(0, start_hbm, start)
    got_head = load(2, stiff_hbm.at[:, :head], stiff.at[:, :head])
    got_orders = load(1, orders_hbm, orders)
    got_out = load(3, out_rows_hbm, out_rows)
    got_counts = load(4, out_counts_hbm, out_counts)
    got_in = load(6, in_rows_hbm, in_rows)

    came_first[...] = jnp.zeros_like(came_first)
    came_second[...] = jnp.zeros_like(came_second)

    teams = n_dom // team
    place = lax.rem(dom, team)
    team_first = dom - place
    column_id = lax.div(dom, team)

    def wrapped(index, size):
        return jnp.where(index >= size, index - size, index)

    def team_mate(step):
        along, across = divmod(step, n_sub)
        return (team_first + wrapped(place + along, team), wrapped(sub + across, n_sub))

    def column_mate(step):
        return (wrapped(column_id + step, teams) * team + place, sub)

    team_steps, column_steps = range(1, team * n_sub), range(1, teams)
    far = [offset for axis_name, offset in DIRECTIONS if axis_name == "dom"]

    barrier = pltpu.get_barrier_semaphore()

    def greet(device):
        pl.semaphore_signal(barrier, inc=1, device_id=device, device_id_type=MESH)

    greetings = len(team_steps) + len(column_steps)
    for step in column_steps:
        greet(column_mate(step))
    for offset in far:
        inside = (dom + offset >= 0) & (dom + offset < n_dom)
        pl.when(inside)(functools.partial(greet, (dom + offset, sub)))
        greetings = greetings + inside.astype(jnp.int32)
    for step in team_steps:
        greet(team_mate(step))

    got_tail = load(5, stiff_hbm.at[:, head:], stiff.at[:, head:])
    got_rhs = load(7, rhs_hbm, rhs)
    got_basis = load(8, basis_hbm, basis)
    got_inverse = load(10, inverse_hbm, inverse)
    got_weights = load(9, weights_hbm, weights)
    got_coarse = load(11, coarse_hbm, coarse)

    def exchange(sent, came, send_sems, recv_sems):
        moves = []
        for index_dir, (axis_name, offset) in enumerate(DIRECTIONS):
            here, length = (sub, n_sub) if axis_name == "sub" else (dom, n_dom)
            there = here + offset
            target = (dom, there) if axis_name == "sub" else (there, sub)
            sends = (there >= 0) & (there < length)
            receives = (here - offset >= 0) & (here - offset < length)
            copy = pltpu.make_async_remote_copy(
                src_ref=sent.at[index_dir],
                dst_ref=came.at[index_dir],
                send_sem=send_sems.at[index_dir],
                recv_sem=recv_sems.at[index_dir],
                device_id=target,
                device_id_type=MESH,
            )
            pl.when(sends)(copy.start)
            moves.append((copy, sends, receives))
        return moves

    def wait_arrivals(moves):
        for copy, _, receives in moves:
            pl.when(receives)(copy.wait_recv)

    def arrived_slots(came):
        return jnp.concatenate([came[j] for j in range(len(DIRECTIONS))], axis=1)

    row_ids = lax.broadcasted_iota(jnp.int32, (head, slots), 0)
    slot_ids = lax.broadcasted_iota(jnp.int32, (1, slots), 1)
    got_out.wait()
    got_counts.wait()
    for j in range(len(DIRECTIONS)):
        wanted = jnp.where(slot_ids < out_counts[:, j : j + 1], out_rows[j], -1)
        picker[:, j * slots : (j + 1) * slots] = (row_ids == wanted).astype(jnp.bfloat16)
    got_in.wait()
    place_ids = lax.broadcasted_iota(jnp.int32, (slots, slots), 1)
    for j in range(len(DIRECTIONS)):
        listed = jnp.broadcast_to(in_rows[j].astype(jnp.float32), (slots, slots)).T
        for t in range(head // slots):
            placer[j * slots : (j + 1) * slots, t * slots : (t + 1) * slots] = (
                listed == (place_ids + t * slots).astype(jnp.float32)
            ).astype(jnp.bfloat16)
    got_start.wait()
    got_orders.wait()
    column_ids = lax.broadcasted_iota(jnp.int32, (1, order_pad), 1)
    row_mask = (column_ids < orders[...]).astype(jnp.float32)
    iterate = start[...] * row_mask
    iterate_bf = iterate.astype(jnp.bfloat16)
    got_head.wait()
    product_head = dot(iterate_bf, stiff[:, :head])
    picked = exact_dot(product_head, picker[...])
    for j in range(len(DIRECTIONS)):
        sent_first[j] = picked[:, j * slots : (j + 1) * slots]
    pl.semaphore_wait(barrier, greetings)
    moves_first = exchange(sent_first, came_first, send_first, recv_first)

    got_rhs.wait()
    got_tail.wait()
    residual_tail = row_mask[:, head:] * (rhs[:, head:] - dot(iterate_bf, stiff[:, head:]))
    results[1, :, head:] = residual_tail
    tail_bf = residual_tail.astype(jnp.bfloat16)
    got_basis.wait()
    basis_pad[...] = jnp.zeros_like(basis_pad)
    basis_pad[:vectors, :] = basis[...]
    slot_basis[...] = dot_t(
        placer[...], basis_pad[:, :head] * row_mask[:, :head].astype(jnp.bfloat16)
    ).astype(jnp.bfloat16)
    own_head = row_mask[:, :head] * (rhs[:, :head] - product_head)
    own_residual = jnp.concatenate([own_head, residual_tail], axis=1)
    own_coarse = exact_dot(own_residual, basis_pad[...], dot_t)
    got_inverse.wait()
    fix_tail = dot(tail_bf, inverse[head:, :])

    wait_arrivals(moves_first)
    arrived = arrived_slots(came_first)
    gathered[me] = own_coarse - exact_dot(arrived, slot_basis[...])

    def share(slabs, device, send_sem, recv_sem):
        pltpu.make_async_remote_copy(
            src_ref=gathered.at[slabs],
            dst_ref=gathered.at[slabs],
            send_sem=send_sem,
            recv_sem=recv_sem,
            device_id=device,
            device_id_type=MESH,
        ).start()

    def wait_slabs(count, sem):
        some = gathered.at[pl.ds(0, count)]
        pltpu.make_async_copy(some, some, sem).wait()

    for step in team_steps:
        share(pl.ds(me, 1), team_mate(step), team_send, team_recv)

    residual_head = own_head - row_mask[:, :head] * exact_dot(arrived, placer[...])
    head_bf = residual_head.astype(jnp.bfloat16)
    results[1, :, :head] = residual_head
    got_weights.wait()
    scale = weights[...].reshape(1, order_pad) * row_mask
    fixed = scale * (fix_tail + dot(head_bf, inverse[:head, :]))
    picked_fix = exact_dot(fixed[:, :head], picker[...])
    base_out = iterate + fixed

    mates = team * n_sub
    wait_slabs(mates - 1, team_recv)
    for step in column_steps:
        share(pl.ds(team_first * n_sub, mates), column_mate(step), column_send, column_recv)

    scaled_basis = scale * basis[...].astype(jnp.float32)
    picked_basis = exact_dot(scaled_basis[:, :head], picker[...])

    got_coarse.wait()
    group = math.lcm(vectors, LANES) // vectors
    lane_ids = lax.broadcasted_iota(jnp.int32, (vectors, LANES), 1)

    def spread(block, carry):
        base = pl.multiple_of(block * group * vectors, LANES)
        tiles = [
            coarse[:, pl.ds(base + t * LANES, LANES)] for t in range(group * vectors // LANES)
        ]
        for r in range(group):
            tile, first = divmod(r * vectors, LANES)
            moved = pltpu.roll(tiles[tile], LANES - first, 1) if first else tiles[tile]
            if first + vectors > LANES:
                following = pltpu.roll(tiles[tile + 1], LANES - first, 1)
                moved = jnp.where(lane_ids < LANES - first, moved, following)
            coarse_pad[block * group + r] = jnp.where(lane_ids < vectors, moved, 0.0)
        return carry

    lax.fori_loop(0, devices // group, spread, 0)

    wait_slabs(devices - mates, column_recv)

    def accumulate(block, sums):
        sums = list(sums)
        for r in range(group):
            d = block * group + r
            terms, rows = gathered[d], coarse_pad[d]
            for l in range(loads):
                sums[l] = sums[l] + terms[l : l + 1, :] * rows
        return tuple(sums)

    sums = tuple(jnp.zeros((vectors, LANES), jnp.float32) for _ in range(loads))
    if devices // group <= 4:
        for block in range(devices // group):
            sums = accumulate(block, sums)
    else:
        sums = lax.fori_loop(0, devices // group, accumulate, sums)
    coarse_columns = [
        jnp.sum(s, axis=1, keepdims=True).astype(jnp.bfloat16).astype(jnp.float32) for s in sums
    ]

    def spanned(block):
        return jnp.concatenate(
            [jnp.sum(c * block, axis=0, keepdims=True) for c in coarse_columns], axis=0
        )

    picked = picked_fix + spanned(picked_basis)
    for j in range(len(DIRECTIONS)):
        sent_second[j] = picked[:, j * slots : (j + 1) * slots]
    moves_second = exchange(sent_second, came_second, send_second, recv_second)

    base_out = base_out + spanned(scaled_basis)
    results[0, :, head:] = base_out[:, head:]
    wait_arrivals(moves_second)
    placed = exact_dot(arrived_slots(came_second), placer[...])
    results[0, :, :head] = base_out[:, :head] + placed
    put_results = pltpu.make_async_copy(results, results_hbm, store_sem)
    put_results.start()

    for copy, sends, _ in moves_first + moves_second:
        pl.when(sends)(copy.wait_send)
    wait_slabs(mates - 1, team_send)
    wait_slabs(devices - mates, column_send)
    put_results.wait()


def per_device(
    n_dom,
    n_sub,
    rhs,
    start,
    stiffness,
    local_inverse,
    basis,
    weights,
    coarse_inverse,
    orders,
    out_rows,
    out_counts,
    in_rows,
):
    loads, order_pad = rhs.shape
    directions, slots = out_rows.shape[1:]
    team = min(t for t in range(1, n_dom + 1) if n_dom % t == 0 and t * t * n_sub >= n_dom)
    vectors = basis.shape[0]
    devices = n_dom * n_sub
    head = -(-(order_pad // 4) // LANES) * LANES
    operands = (
        rhs,
        start,
        stiffness,
        local_inverse,
        basis,
        weights,
        coarse_inverse,
        orders.reshape(1, 1),
        out_rows.transpose(1, 0, 2),
        out_counts,
        in_rows.transpose(1, 0, 2),
    )
    f32 = jnp.float32
    shared = pltpu.VMEM((directions, loads, slots), f32)
    dma = pltpu.SemaphoreType.DMA
    in_hbm = pl.BlockSpec(memory_space=pltpu.HBM)
    both = jax.ShapeDtypeStruct((2, loads, order_pad), f32)
    results = pl.pallas_call(
        functools.partial(kernel, n_dom, n_sub, team),
        out_shape=both,
        in_specs=[in_hbm] * len(operands),
        out_specs=in_hbm,
        scratch_shapes=[pltpu.VMEM(x.shape, x.dtype) for x in operands]
        + [
            pltpu.VMEM((head, directions * slots), jnp.bfloat16),
            pltpu.VMEM((directions * slots, head), jnp.bfloat16),
            pltpu.VMEM((LANES, order_pad), jnp.bfloat16),
            pltpu.VMEM((directions * slots, LANES), jnp.bfloat16),
            pltpu.VMEM((devices, vectors, LANES), f32),
            shared,
            shared,
            shared,
            shared,
            pltpu.VMEM((devices, loads, LANES), f32),
            pltpu.VMEM((2, loads, order_pad), f32),
            dma((12,)),
            dma,
            dma((directions,)),
            dma((directions,)),
            dma((directions,)),
            dma((directions,)),
            dma,
            dma,
            dma,
            dma,
        ],
        compiler_params=pltpu.CompilerParams(
            collective_id=0, has_side_effects=True, vmem_limit_bytes=63 * 1024 * 1024
        ),
    )(*operands)
    return results[0], results[1]


def solution(mesh):
    return jax.shard_map(
        functools.partial(per_device, mesh.shape["dom"], mesh.shape["sub"]),
        mesh=mesh,
        in_specs=(
            P(None, ("dom", "sub")),
            P(None, ("dom", "sub")),
            P(("dom", "sub"), None),
            P(("dom", "sub"), None),
            P(None, ("dom", "sub")),
            P(("dom", "sub")),
            P(("dom", "sub"), None),
            P(("dom", "sub")),
            P(("dom", "sub"), None, None),
            P(("dom", "sub"), None),
            P(("dom", "sub"), None, None),
        ),
        out_specs=(P(None, ("dom", "sub")), P(None, ("dom", "sub"))),
        check_vma=False,
    )
```

```python
import functools
import math

import jax
import jax.numpy as jnp
from jax import lax
from jax.experimental import pallas as pl
from jax.experimental.pallas import tpu as pltpu
from jax.sharding import PartitionSpec as P

DIRECTIONS = (("sub", 1), ("sub", -1), ("dom", 1), ("dom", -1), ("dom", 2), ("dom", -2))
MESH = pl.DeviceIdType.MESH
LANES = 128


def halves(x):
    high = x.astype(jnp.bfloat16).astype(jnp.float32)
    return jnp.concatenate([high, x - high], axis=0).astype(jnp.bfloat16)


def dot(a, b):
    return jnp.dot(a, b, preferred_element_type=jnp.float32)


def dot_t(a, b):
    return lax.dot_general(a, b, (((1,), (1,)), ((), ())), preferred_element_type=jnp.float32)


def exact_dot(x, picker, by=dot):
    rows = x.shape[0]
    both = by(halves(x), picker)
    return both[:rows] + both[rows:]


def kernel(
    n_dom,
    n_sub,
    team,
    rhs_hbm,
    start_hbm,
    stiff_hbm,
    inverse_hbm,
    basis_hbm,
    weights_hbm,
    coarse_hbm,
    orders_hbm,
    out_rows_hbm,
    out_counts_hbm,
    in_rows_hbm,
    results,
    rhs,
    start,
    stiff,
    inverse,
    basis,
    weights,
    coarse,
    orders,
    out_rows,
    out_counts,
    in_rows,
    picker,
    placer,
    basis_pad,
    slot_basis,
    coarse_pad,
    sent_first,
    sent_second,
    came_first,
    came_second,
    gathered,
    load_sems,
    send_first,
    recv_first,
    send_second,
    recv_second,
    team_send,
    team_recv,
    column_send,
    column_recv,
):
    devices = n_dom * n_sub
    loads, order_pad = rhs.shape
    slots = out_rows.shape[2]
    vectors = basis.shape[0]
    head = placer.shape[1]
    dom, sub = lax.axis_index("dom"), lax.axis_index("sub")
    me = dom * n_sub + sub

    def load(index, source, target):
        copy = pltpu.make_async_copy(source, target, load_sems.at[index])
        copy.start()
        return copy

    got_start = load(0, start_hbm, start)
    got_head = load(2, stiff_hbm.at[:, :head], stiff.at[:, :head])
    got_orders = load(1, orders_hbm, orders)
    got_out = load(3, out_rows_hbm, out_rows)
    got_counts = load(4, out_counts_hbm, out_counts)
    got_in = load(6, in_rows_hbm, in_rows)

    came_first[...] = jnp.zeros_like(came_first)
    came_second[...] = jnp.zeros_like(came_second)

    teams = n_dom // team
    place = lax.rem(dom, team)
    team_first = dom - place
    column_id = lax.div(dom, team)

    def wrapped(index, size):
        return jnp.where(index >= size, index - size, index)

    def team_mate(step):
        along, across = divmod(step, n_sub)
        return (team_first + wrapped(place + along, team), wrapped(sub + across, n_sub))

    def column_mate(step):
        return (wrapped(column_id + step, teams) * team + place, sub)

    team_steps, column_steps = range(1, team * n_sub), range(1, teams)
    far = [offset for axis_name, offset in DIRECTIONS if axis_name == "dom"]

    barrier = pltpu.get_barrier_semaphore()

    def greet(device):
        pl.semaphore_signal(barrier, inc=1, device_id=device, device_id_type=MESH)

    greetings = len(team_steps) + len(column_steps)
    for step in column_steps:
        greet(column_mate(step))
    for offset in far:
        inside = (dom + offset >= 0) & (dom + offset < n_dom)
        pl.when(inside)(functools.partial(greet, (dom + offset, sub)))
        greetings = greetings + inside.astype(jnp.int32)
    for step in team_steps:
        greet(team_mate(step))

    got_tail = load(5, stiff_hbm.at[:, head:], stiff.at[:, head:])
    got_rhs = load(7, rhs_hbm, rhs)
    got_basis = load(8, basis_hbm, basis)
    got_inverse = load(10, inverse_hbm, inverse)
    got_weights = load(9, weights_hbm, weights)
    got_coarse = load(11, coarse_hbm, coarse)

    def exchange(sent, came, send_sems, recv_sems):
        moves = []
        for index_dir, (axis_name, offset) in enumerate(DIRECTIONS):
            here, length = (sub, n_sub) if axis_name == "sub" else (dom, n_dom)
            there = here + offset
            target = (dom, there) if axis_name == "sub" else (there, sub)
            sends = (there >= 0) & (there < length)
            receives = (here - offset >= 0) & (here - offset < length)
            copy = pltpu.make_async_remote_copy(
                src_ref=sent.at[index_dir],
                dst_ref=came.at[index_dir],
                send_sem=send_sems.at[index_dir],
                recv_sem=recv_sems.at[index_dir],
                device_id=target,
                device_id_type=MESH,
            )
            pl.when(sends)(copy.start)
            moves.append((copy, sends, receives))
        return moves

    def wait_arrivals(moves):
        for copy, _, receives in moves:
            pl.when(receives)(copy.wait_recv)

    def arrived_slots(came):
        return jnp.concatenate([came[j] for j in range(len(DIRECTIONS))], axis=1)

    row_ids = lax.broadcasted_iota(jnp.int32, (head, slots), 0)
    slot_ids = lax.broadcasted_iota(jnp.int32, (1, slots), 1)
    got_out.wait()
    got_counts.wait()
    for j in range(len(DIRECTIONS)):
        wanted = jnp.where(slot_ids < out_counts[:, j : j + 1], out_rows[j], -1)
        picker[:, j * slots : (j + 1) * slots] = (row_ids == wanted).astype(jnp.bfloat16)
    got_start.wait()
    got_orders.wait()
    column_ids = lax.broadcasted_iota(jnp.int32, (1, order_pad), 1)
    row_mask = (column_ids < orders[...]).astype(jnp.float32)
    iterate = start[...] * row_mask
    iterate_bf = iterate.astype(jnp.bfloat16)
    got_head.wait()
    product_head = dot(iterate_bf, stiff[:, :head])
    picked = exact_dot(product_head, picker[...])
    for j in range(len(DIRECTIONS)):
        sent_first[j] = picked[:, j * slots : (j + 1) * slots]
    pl.semaphore_wait(barrier, greetings)
    moves_first = exchange(sent_first, came_first, send_first, recv_first)

    got_in.wait()
    place_ids = lax.broadcasted_iota(jnp.int32, (slots, slots), 1)
    for j in range(len(DIRECTIONS)):
        listed = jnp.broadcast_to(in_rows[j].astype(jnp.float32), (slots, slots)).T
        for t in range(head // slots):
            placer[j * slots : (j + 1) * slots, t * slots : (t + 1) * slots] = (
                listed == (place_ids + t * slots).astype(jnp.float32)
            ).astype(jnp.bfloat16)
    got_rhs.wait()
    got_tail.wait()
    residual_tail = row_mask[:, head:] * (rhs[:, head:] - dot(iterate_bf, stiff[:, head:]))
    results[1, :, head:] = residual_tail
    got_basis.wait()
    basis_pad[...] = jnp.zeros_like(basis_pad)
    basis_pad[:vectors, :] = basis[...]
    slot_basis[...] = dot_t(
        placer[...], basis_pad[:, :head] * row_mask[:, :head].astype(jnp.bfloat16)
    ).astype(jnp.bfloat16)
    own_head = row_mask[:, :head] * (rhs[:, :head] - product_head)
    own_residual = jnp.concatenate([own_head, residual_tail], axis=1)
    own_coarse = exact_dot(own_residual, basis_pad[...], dot_t)

    wait_arrivals(moves_first)
    arrived = arrived_slots(came_first)
    gathered[me] = own_coarse - exact_dot(arrived, slot_basis[...])

    def share(slabs, device, send_sem, recv_sem):
        pltpu.make_async_remote_copy(
            src_ref=gathered.at[slabs],
            dst_ref=gathered.at[slabs],
            send_sem=send_sem,
            recv_sem=recv_sem,
            device_id=device,
            device_id_type=MESH,
        ).start()

    def wait_slabs(count, sem):
        some = gathered.at[pl.ds(0, count)]
        pltpu.make_async_copy(some, some, sem).wait()

    for step in team_steps:
        share(pl.ds(me, 1), team_mate(step), team_send, team_recv)

    residual_head = own_head - row_mask[:, :head] * exact_dot(arrived, placer[...])
    residual_bf = jnp.concatenate([residual_head, residual_tail], axis=1).astype(jnp.bfloat16)
    results[1, :, :head] = residual_head
    got_weights.wait()
    scale = weights[...].reshape(1, order_pad) * row_mask
    got_inverse.wait()
    fixed = scale * dot(residual_bf, inverse[...])
    picked_fix = exact_dot(fixed[:, :head], picker[...])
    base_out = iterate + fixed

    mates = team * n_sub
    wait_slabs(mates - 1, team_recv)
    for step in column_steps:
        share(pl.ds(team_first * n_sub, mates), column_mate(step), column_send, column_recv)

    scaled_basis = scale * basis[...].astype(jnp.float32)
    picked_basis = exact_dot(scaled_basis[:, :head], picker[...])

    got_coarse.wait()
    group = math.lcm(vectors, LANES) // vectors
    lane_ids = lax.broadcasted_iota(jnp.int32, (vectors, LANES), 1)

    def spread(block, carry):
        base = pl.multiple_of(block * group * vectors, LANES)
        tiles = [
            coarse[:, pl.ds(base + t * LANES, LANES)] for t in range(group * vectors // LANES)
        ]
        for r in range(group):
            tile, first = divmod(r * vectors, LANES)
            moved = pltpu.roll(tiles[tile], LANES - first, 1) if first else tiles[tile]
            if first + vectors > LANES:
                following = pltpu.roll(tiles[tile + 1], LANES - first, 1)
                moved = jnp.where(lane_ids < LANES - first, moved, following)
            coarse_pad[block * group + r] = jnp.where(lane_ids < vectors, moved, 0.0)
        return carry

    lax.fori_loop(0, devices // group, spread, 0)

    wait_slabs(devices - mates, column_recv)

    def accumulate(block, sums):
        sums = list(sums)
        for r in range(group):
            d = block * group + r
            terms, rows = gathered[d], coarse_pad[d]
            for l in range(loads):
                sums[l] = sums[l] + terms[l : l + 1, :] * rows
        return tuple(sums)

    sums = tuple(jnp.zeros((vectors, LANES), jnp.float32) for _ in range(loads))
    if devices // group <= 4:
        for block in range(devices // group):
            sums = accumulate(block, sums)
    else:
        sums = lax.fori_loop(0, devices // group, accumulate, sums)
    coarse_columns = [
        jnp.sum(s, axis=1, keepdims=True).astype(jnp.bfloat16).astype(jnp.float32) for s in sums
    ]

    def spanned(block):
        return jnp.concatenate(
            [jnp.sum(c * block, axis=0, keepdims=True) for c in coarse_columns], axis=0
        )

    picked = picked_fix + spanned(picked_basis)
    for j in range(len(DIRECTIONS)):
        sent_second[j] = picked[:, j * slots : (j + 1) * slots]
    moves_second = exchange(sent_second, came_second, send_second, recv_second)

    base_out = base_out + spanned(scaled_basis)
    results[0, :, head:] = base_out[:, head:]
    wait_arrivals(moves_second)
    placed = exact_dot(arrived_slots(came_second), placer[...])
    results[0, :, :head] = base_out[:, :head] + placed

    for copy, sends, _ in moves_first + moves_second:
        pl.when(sends)(copy.wait_send)
    wait_slabs(mates - 1, team_send)
    wait_slabs(devices - mates, column_send)


def per_device(
    n_dom,
    n_sub,
    rhs,
    start,
    stiffness,
    local_inverse,
    basis,
    weights,
    coarse_inverse,
    orders,
    out_rows,
    out_counts,
    in_rows,
):
    loads, order_pad = rhs.shape
    directions, slots = out_rows.shape[1:]
    team = min(t for t in range(1, n_dom + 1) if n_dom % t == 0 and t * t * n_sub >= n_dom)
    vectors = basis.shape[0]
    devices = n_dom * n_sub
    head = -(-(order_pad // 4) // LANES) * LANES
    operands = (
        rhs,
        start,
        stiffness,
        local_inverse,
        basis,
        weights,
        coarse_inverse,
        orders.reshape(1, 1),
        out_rows.transpose(1, 0, 2),
        out_counts,
        in_rows.transpose(1, 0, 2),
    )
    f32 = jnp.float32
    shared = pltpu.VMEM((directions, loads, slots), f32)
    dma = pltpu.SemaphoreType.DMA
    in_hbm = pl.BlockSpec(memory_space=pltpu.HBM)
    both = pltpu.VMEM((2, loads, order_pad), f32)
    results = pl.pallas_call(
        functools.partial(kernel, n_dom, n_sub, team),
        out_shape=both,
        in_specs=[in_hbm] * len(operands),
        out_specs=pl.BlockSpec(memory_space=pltpu.VMEM),
        scratch_shapes=[pltpu.VMEM(x.shape, x.dtype) for x in operands]
        + [
            pltpu.VMEM((head, directions * slots), jnp.bfloat16),
            pltpu.VMEM((directions * slots, head), jnp.bfloat16),
            pltpu.VMEM((LANES, order_pad), jnp.bfloat16),
            pltpu.VMEM((directions * slots, LANES), jnp.bfloat16),
            pltpu.VMEM((devices, vectors, LANES), f32),
            shared,
            shared,
            shared,
            shared,
            pltpu.VMEM((devices, loads, LANES), f32),
            dma((12,)),
            dma((directions,)),
            dma((directions,)),
            dma((directions,)),
            dma((directions,)),
            dma,
            dma,
            dma,
            dma,
        ],
        compiler_params=pltpu.CompilerParams(
            collective_id=0, has_side_effects=True, vmem_limit_bytes=63 * 1024 * 1024
        ),
    )(*operands)
    return results[0], results[1]


def solution(mesh):
    return jax.shard_map(
        functools.partial(per_device, mesh.shape["dom"], mesh.shape["sub"]),
        mesh=mesh,
        in_specs=(
            P(None, ("dom", "sub")),
            P(None, ("dom", "sub")),
            P(("dom", "sub"), None),
            P(("dom", "sub"), None),
            P(None, ("dom", "sub")),
            P(("dom", "sub")),
            P(("dom", "sub"), None),
            P(("dom", "sub")),
            P(("dom", "sub"), None, None),
            P(("dom", "sub"), None),
            P(("dom", "sub"), None, None),
        ),
        out_specs=(P(None, ("dom", "sub")), P(None, ("dom", "sub"))),
        check_vma=False,
    )
```

```python
import functools
import math

import jax
import jax.numpy as jnp
from jax import lax
from jax.experimental import pallas as pl
from jax.experimental.pallas import tpu as pltpu
from jax.sharding import PartitionSpec as P

DIRECTIONS = (("sub", 1), ("sub", -1), ("dom", 1), ("dom", -1), ("dom", 2), ("dom", -2))
MESH = pl.DeviceIdType.MESH
LANES = 128


def halves(x):
    high = x.astype(jnp.bfloat16).astype(jnp.float32)
    return jnp.concatenate([high, x - high], axis=0).astype(jnp.bfloat16)


def dot(a, b):
    return jnp.dot(a, b, preferred_element_type=jnp.float32)


def dot_t(a, b):
    return lax.dot_general(a, b, (((1,), (1,)), ((), ())), preferred_element_type=jnp.float32)


def exact_dot(x, picker, by=dot):
    rows = x.shape[0]
    both = by(halves(x), picker)
    return both[:rows] + both[rows:]


def kernel(
    n_dom,
    n_sub,
    team,
    rhs_hbm,
    start_hbm,
    stiff_hbm,
    inverse_hbm,
    basis_hbm,
    weights_hbm,
    coarse_hbm,
    orders_hbm,
    out_rows_hbm,
    out_counts_hbm,
    in_rows_hbm,
    results,
    rhs,
    start,
    stiff,
    inverse,
    basis,
    weights,
    coarse,
    orders,
    out_rows,
    out_counts,
    in_rows,
    picker,
    placer,
    basis_pad,
    slot_basis,
    coarse_pad,
    sent_first,
    sent_second,
    came_first,
    came_second,
    gathered,
    load_sems,
    send_first,
    recv_first,
    send_second,
    recv_second,
    team_send,
    team_recv,
    column_send,
    column_recv,
):
    devices = n_dom * n_sub
    loads, order_pad = rhs.shape
    slots = out_rows.shape[2]
    vectors = basis.shape[0]
    head = placer.shape[1]
    dom, sub = lax.axis_index("dom"), lax.axis_index("sub")
    me = dom * n_sub + sub

    def load(index, source, target):
        copy = pltpu.make_async_copy(source, target, load_sems.at[index])
        copy.start()
        return copy

    got_head = load(2, stiff_hbm.at[:, :head], stiff.at[:, :head])
    got_start = load(0, start_hbm, start)
    got_orders = load(1, orders_hbm, orders)
    got_out = load(3, out_rows_hbm, out_rows)
    got_counts = load(4, out_counts_hbm, out_counts)
    got_in = load(6, in_rows_hbm, in_rows)

    came_first[...] = jnp.zeros_like(came_first)
    came_second[...] = jnp.zeros_like(came_second)

    teams = n_dom // team
    place = lax.rem(dom, team)
    team_first = dom - place
    column_id = lax.div(dom, team)

    def wrapped(index, size):
        return jnp.where(index >= size, index - size, index)

    def team_mate(step):
        along, across = divmod(step, n_sub)
        return (team_first + wrapped(place + along, team), wrapped(sub + across, n_sub))

    def column_mate(step):
        return (wrapped(column_id + step, teams) * team + place, sub)

    team_steps, column_steps = range(1, team * n_sub), range(1, teams)
    far = [offset for axis_name, offset in DIRECTIONS if axis_name == "dom"]

    barrier = pltpu.get_barrier_semaphore()

    def greet(device):
        pl.semaphore_signal(barrier, inc=1, device_id=device, device_id_type=MESH)

    greetings = len(team_steps) + len(column_steps)
    for step in column_steps:
        greet(column_mate(step))
    for offset in far:
        inside = (dom + offset >= 0) & (dom + offset < n_dom)
        pl.when(inside)(functools.partial(greet, (dom + offset, sub)))
        greetings = greetings + inside.astype(jnp.int32)
    for step in team_steps:
        greet(team_mate(step))

    got_tail = load(5, stiff_hbm.at[:, head:], stiff.at[:, head:])
    got_rhs = load(7, rhs_hbm, rhs)
    got_basis = load(8, basis_hbm, basis)
    got_inverse = load(10, inverse_hbm, inverse)
    got_weights = load(9, weights_hbm, weights)
    got_coarse = load(11, coarse_hbm, coarse)

    def exchange(sent, came, send_sems, recv_sems):
        moves = []
        for index_dir, (axis_name, offset) in enumerate(DIRECTIONS):
            here, length = (sub, n_sub) if axis_name == "sub" else (dom, n_dom)
            there = here + offset
            target = (dom, there) if axis_name == "sub" else (there, sub)
            sends = (there >= 0) & (there < length)
            receives = (here - offset >= 0) & (here - offset < length)
            copy = pltpu.make_async_remote_copy(
                src_ref=sent.at[index_dir],
                dst_ref=came.at[index_dir],
                send_sem=send_sems.at[index_dir],
                recv_sem=recv_sems.at[index_dir],
                device_id=target,
                device_id_type=MESH,
            )
            pl.when(sends)(copy.start)
            moves.append((copy, sends, receives))
        return moves

    def wait_arrivals(moves):
        for copy, _, receives in moves:
            pl.when(receives)(copy.wait_recv)

    def arrived_slots(came):
        return jnp.concatenate([came[j] for j in range(len(DIRECTIONS))], axis=1)

    row_ids = lax.broadcasted_iota(jnp.int32, (head, slots), 0)
    slot_ids = lax.broadcasted_iota(jnp.int32, (1, slots), 1)
    got_out.wait()
    got_counts.wait()
    for j in range(len(DIRECTIONS)):
        wanted = jnp.where(slot_ids < out_counts[:, j : j + 1], out_rows[j], -1)
        picker[:, j * slots : (j + 1) * slots] = (row_ids == wanted).astype(jnp.bfloat16)
    got_start.wait()
    got_orders.wait()
    column_ids = lax.broadcasted_iota(jnp.int32, (1, order_pad), 1)
    row_mask = (column_ids < orders[...]).astype(jnp.float32)
    iterate = start[...] * row_mask
    iterate_bf = iterate.astype(jnp.bfloat16)
    got_head.wait()
    product_head = dot(iterate_bf, stiff[:, :head])
    picked = exact_dot(product_head, picker[...])
    for j in range(len(DIRECTIONS)):
        sent_first[j] = picked[:, j * slots : (j + 1) * slots]
    pl.semaphore_wait(barrier, greetings)
    moves_first = exchange(sent_first, came_first, send_first, recv_first)

    got_in.wait()
    place_ids = lax.broadcasted_iota(jnp.int32, (slots, slots), 1)
    for j in range(len(DIRECTIONS)):
        listed = jnp.broadcast_to(in_rows[j].astype(jnp.float32), (slots, slots)).T
        for t in range(head // slots):
            placer[j * slots : (j + 1) * slots, t * slots : (t + 1) * slots] = (
                listed == (place_ids + t * slots).astype(jnp.float32)
            ).astype(jnp.bfloat16)
    got_rhs.wait()
    got_tail.wait()
    residual_tail = row_mask[:, head:] * (rhs[:, head:] - dot(iterate_bf, stiff[:, head:]))
    results[1, :, head:] = residual_tail
    got_basis.wait()
    basis_pad[...] = jnp.zeros_like(basis_pad)
    basis_pad[:vectors, :] = basis[...]
    slot_basis[...] = dot_t(
        placer[...], basis_pad[:, :head] * row_mask[:, :head].astype(jnp.bfloat16)
    ).astype(jnp.bfloat16)
    own_head = row_mask[:, :head] * (rhs[:, :head] - product_head)
    own_residual = jnp.concatenate([own_head, residual_tail], axis=1)
    own_coarse = exact_dot(own_residual, basis_pad[...], dot_t)

    wait_arrivals(moves_first)
    arrived = arrived_slots(came_first)
    gathered[me] = own_coarse - exact_dot(arrived, slot_basis[...])

    def share(slabs, device, send_sem, recv_sem):
        pltpu.make_async_remote_copy(
            src_ref=gathered.at[slabs],
            dst_ref=gathered.at[slabs],
            send_sem=send_sem,
            recv_sem=recv_sem,
            device_id=device,
            device_id_type=MESH,
        ).start()

    def wait_slabs(count, sem):
        some = gathered.at[pl.ds(0, count)]
        pltpu.make_async_copy(some, some, sem).wait()

    for step in team_steps:
        share(pl.ds(me, 1), team_mate(step), team_send, team_recv)

    residual_head = own_head - row_mask[:, :head] * exact_dot(arrived, placer[...])
    residual_bf = jnp.concatenate([residual_head, residual_tail], axis=1).astype(jnp.bfloat16)
    results[1, :, :head] = residual_head
    got_weights.wait()
    scale = weights[...].reshape(1, order_pad) * row_mask
    got_inverse.wait()
    fixed = scale * dot(residual_bf, inverse[...])
    picked_fix = exact_dot(fixed[:, :head], picker[...])
    base_out = iterate + fixed

    mates = team * n_sub
    wait_slabs(mates - 1, team_recv)
    for step in column_steps:
        share(pl.ds(team_first * n_sub, mates), column_mate(step), column_send, column_recv)

    scaled_basis = scale * basis[...].astype(jnp.float32)
    picked_basis = exact_dot(scaled_basis[:, :head], picker[...])

    got_coarse.wait()
    group = math.lcm(vectors, LANES) // vectors
    lane_ids = lax.broadcasted_iota(jnp.int32, (vectors, LANES), 1)

    def spread(block, carry):
        base = pl.multiple_of(block * group * vectors, LANES)
        tiles = [
            coarse[:, pl.ds(base + t * LANES, LANES)] for t in range(group * vectors // LANES)
        ]
        for r in range(group):
            tile, first = divmod(r * vectors, LANES)
            moved = pltpu.roll(tiles[tile], LANES - first, 1) if first else tiles[tile]
            if first + vectors > LANES:
                following = pltpu.roll(tiles[tile + 1], LANES - first, 1)
                moved = jnp.where(lane_ids < LANES - first, moved, following)
            coarse_pad[block * group + r] = jnp.where(lane_ids < vectors, moved, 0.0)
        return carry

    lax.fori_loop(0, devices // group, spread, 0)

    wait_slabs(devices - mates, column_recv)

    def accumulate(block, sums):
        sums = list(sums)
        for r in range(group):
            d = block * group + r
            terms, rows = gathered[d], coarse_pad[d]
            for l in range(loads):
                sums[l] = sums[l] + terms[l : l + 1, :] * rows
        return tuple(sums)

    sums = tuple(jnp.zeros((vectors, LANES), jnp.float32) for _ in range(loads))
    if devices // group <= 4:
        for block in range(devices // group):
            sums = accumulate(block, sums)
    else:
        sums = lax.fori_loop(0, devices // group, accumulate, sums)
    coarse_columns = [
        jnp.sum(s, axis=1, keepdims=True).astype(jnp.bfloat16).astype(jnp.float32) for s in sums
    ]

    def spanned(block):
        return jnp.concatenate(
            [jnp.sum(c * block, axis=0, keepdims=True) for c in coarse_columns], axis=0
        )

    picked = picked_fix + spanned(picked_basis)
    for j in range(len(DIRECTIONS)):
        sent_second[j] = picked[:, j * slots : (j + 1) * slots]
    moves_second = exchange(sent_second, came_second, send_second, recv_second)

    base_out = base_out + spanned(scaled_basis)
    results[0, :, head:] = base_out[:, head:]
    for copy, sends, _ in moves_first + moves_second:
        pl.when(sends)(copy.wait_send)
    wait_slabs(mates - 1, team_send)
    wait_slabs(devices - mates, column_send)
    wait_arrivals(moves_second)
    placed = exact_dot(arrived_slots(came_second), placer[...])
    results[0, :, :head] = base_out[:, :head] + placed


def per_device(
    n_dom,
    n_sub,
    rhs,
    start,
    stiffness,
    local_inverse,
    basis,
    weights,
    coarse_inverse,
    orders,
    out_rows,
    out_counts,
    in_rows,
):
    loads, order_pad = rhs.shape
    directions, slots = out_rows.shape[1:]
    team = min(t for t in range(1, n_dom + 1) if n_dom % t == 0 and t * t * n_sub >= n_dom)
    vectors = basis.shape[0]
    devices = n_dom * n_sub
    head = -(-(order_pad // 4) // LANES) * LANES
    operands = (
        rhs,
        start,
        stiffness,
        local_inverse,
        basis,
        weights,
        coarse_inverse,
        orders.reshape(1, 1),
        out_rows.transpose(1, 0, 2),
        out_counts,
        in_rows.transpose(1, 0, 2),
    )
    f32 = jnp.float32
    shared = pltpu.VMEM((directions, loads, slots), f32)
    dma = pltpu.SemaphoreType.DMA
    in_hbm = pl.BlockSpec(memory_space=pltpu.HBM)
    both = pltpu.VMEM((2, loads, order_pad), f32)
    results = pl.pallas_call(
        functools.partial(kernel, n_dom, n_sub, team),
        out_shape=both,
        in_specs=[in_hbm] * len(operands),
        out_specs=pl.BlockSpec(memory_space=pltpu.VMEM),
        scratch_shapes=[pltpu.VMEM(x.shape, x.dtype) for x in operands]
        + [
            pltpu.VMEM((head, directions * slots), jnp.bfloat16),
            pltpu.VMEM((directions * slots, head), jnp.bfloat16),
            pltpu.VMEM((LANES, order_pad), jnp.bfloat16),
            pltpu.VMEM((directions * slots, LANES), jnp.bfloat16),
            pltpu.VMEM((devices, vectors, LANES), f32),
            shared,
            shared,
            shared,
            shared,
            pltpu.VMEM((devices, loads, LANES), f32),
            dma((12,)),
            dma((directions,)),
            dma((directions,)),
            dma((directions,)),
            dma((directions,)),
            dma,
            dma,
            dma,
            dma,
        ],
        compiler_params=pltpu.CompilerParams(
            collective_id=0, has_side_effects=True, vmem_limit_bytes=63 * 1024 * 1024
        ),
    )(*operands)
    return results[0], results[1]


def solution(mesh):
    return jax.shard_map(
        functools.partial(per_device, mesh.shape["dom"], mesh.shape["sub"]),
        mesh=mesh,
        in_specs=(
            P(None, ("dom", "sub")),
            P(None, ("dom", "sub")),
            P(("dom", "sub"), None),
            P(("dom", "sub"), None),
            P(None, ("dom", "sub")),
            P(("dom", "sub")),
            P(("dom", "sub"), None),
            P(("dom", "sub")),
            P(("dom", "sub"), None, None),
            P(("dom", "sub"), None),
            P(("dom", "sub"), None, None),
        ),
        out_specs=(P(None, ("dom", "sub")), P(None, ("dom", "sub"))),
        check_vma=False,
    )
```

```python
import functools
import math

import jax
import jax.numpy as jnp
from jax import lax
from jax.experimental import pallas as pl
from jax.experimental.pallas import tpu as pltpu
from jax.sharding import PartitionSpec as P

DIRECTIONS = (("sub", 1), ("sub", -1), ("dom", 1), ("dom", -1), ("dom", 2), ("dom", -2))
MESH = pl.DeviceIdType.MESH
LANES = 128


def halves(x):
    high = x.astype(jnp.bfloat16).astype(jnp.float32)
    return jnp.concatenate([high, x - high], axis=0).astype(jnp.bfloat16)


def dot(a, b):
    return jnp.dot(a, b, preferred_element_type=jnp.float32)


def dot_t(a, b):
    return lax.dot_general(a, b, (((1,), (1,)), ((), ())), preferred_element_type=jnp.float32)


def exact_dot(x, picker, by=dot):
    rows = x.shape[0]
    both = by(halves(x), picker)
    return both[:rows] + both[rows:]


def kernel(
    n_dom,
    n_sub,
    team,
    rhs_hbm,
    start_hbm,
    stiff_hbm,
    inverse_hbm,
    basis_hbm,
    weights_hbm,
    coarse_hbm,
    orders_hbm,
    out_rows_hbm,
    out_counts_hbm,
    in_rows_hbm,
    results,
    rhs,
    start,
    stiff,
    inverse,
    basis,
    weights,
    coarse,
    orders,
    out_rows,
    out_counts,
    in_rows,
    picker,
    placer,
    basis_pad,
    slot_basis,
    coarse_pad,
    sent_first,
    sent_second,
    came_first,
    came_second,
    gathered,
    load_sems,
    send_first,
    recv_first,
    send_second,
    recv_second,
    team_send,
    team_recv,
    column_send,
    column_recv,
):
    devices = n_dom * n_sub
    loads, order_pad = rhs.shape
    slots = out_rows.shape[2]
    vectors = basis.shape[0]
    head = placer.shape[1]
    dom, sub = lax.axis_index("dom"), lax.axis_index("sub")
    me = dom * n_sub + sub

    def load(index, source, target):
        copy = pltpu.make_async_copy(source, target, load_sems.at[index])
        copy.start()
        return copy

    got_head = load(2, stiff_hbm.at[:, :head], stiff.at[:, :head])
    got_start = load(0, start_hbm, start)
    got_orders = load(1, orders_hbm, orders)
    got_out = load(3, out_rows_hbm, out_rows)
    got_counts = load(4, out_counts_hbm, out_counts)
    got_in = load(6, in_rows_hbm, in_rows)

    came_first[...] = jnp.zeros_like(came_first)
    came_second[...] = jnp.zeros_like(came_second)

    teams = n_dom // team
    place = lax.rem(dom, team)
    team_first = dom - place
    column_id = lax.div(dom, team)

    def wrapped(index, size):
        return jnp.where(index >= size, index - size, index)

    def team_mate(step):
        along, across = divmod(step, n_sub)
        return (team_first + wrapped(place + along, team), wrapped(sub + across, n_sub))

    def column_mate(step):
        return (wrapped(column_id + step, teams) * team + place, sub)

    team_steps, column_steps = range(1, team * n_sub), range(1, teams)
    far = [offset for axis_name, offset in DIRECTIONS if axis_name == "dom"]

    barrier = pltpu.get_barrier_semaphore()

    def greet(device):
        pl.semaphore_signal(barrier, inc=1, device_id=device, device_id_type=MESH)

    greetings = len(team_steps) + len(column_steps)
    for step in column_steps:
        greet(column_mate(step))
    for offset in far:
        inside = (dom + offset >= 0) & (dom + offset < n_dom)
        pl.when(inside)(functools.partial(greet, (dom + offset, sub)))
        greetings = greetings + inside.astype(jnp.int32)
    for step in team_steps:
        greet(team_mate(step))

    got_tail = load(5, stiff_hbm.at[:, head:], stiff.at[:, head:])
    got_rhs = load(7, rhs_hbm, rhs)
    got_basis = load(8, basis_hbm, basis)
    got_inverse = load(10, inverse_hbm, inverse)
    got_weights = load(9, weights_hbm, weights)
    got_coarse = load(11, coarse_hbm, coarse)

    def exchange(sent, came, send_sems, recv_sems):
        moves = []
        for index_dir, (axis_name, offset) in enumerate(DIRECTIONS):
            here, length = (sub, n_sub) if axis_name == "sub" else (dom, n_dom)
            there = here + offset
            target = (dom, there) if axis_name == "sub" else (there, sub)
            sends = (there >= 0) & (there < length)
            receives = (here - offset >= 0) & (here - offset < length)
            copy = pltpu.make_async_remote_copy(
                src_ref=sent.at[index_dir],
                dst_ref=came.at[index_dir],
                send_sem=send_sems.at[index_dir],
                recv_sem=recv_sems.at[index_dir],
                device_id=target,
                device_id_type=MESH,
            )
            pl.when(sends)(copy.start)
            moves.append((copy, sends, receives))
        return moves

    def wait_arrivals(moves):
        for copy, _, receives in moves:
            pl.when(receives)(copy.wait_recv)

    def arrived_slots(came):
        return jnp.concatenate([came[j] for j in range(len(DIRECTIONS))], axis=1)

    row_ids = lax.broadcasted_iota(jnp.int32, (head, slots), 0)
    slot_ids = lax.broadcasted_iota(jnp.int32, (1, slots), 1)
    got_out.wait()
    got_counts.wait()
    for j in range(len(DIRECTIONS)):
        wanted = jnp.where(slot_ids < out_counts[:, j : j + 1], out_rows[j], -1)
        picker[:, j * slots : (j + 1) * slots] = (row_ids == wanted).astype(jnp.bfloat16)
    got_start.wait()
    got_orders.wait()
    column_ids = lax.broadcasted_iota(jnp.int32, (1, order_pad), 1)
    row_mask = (column_ids < orders[...]).astype(jnp.float32)
    iterate = start[...] * row_mask
    iterate_bf = iterate.astype(jnp.bfloat16)
    got_head.wait()
    product_head = dot(iterate_bf, stiff[:, :head])
    picked = exact_dot(product_head, picker[...])
    for j in range(len(DIRECTIONS)):
        sent_first[j] = picked[:, j * slots : (j + 1) * slots]
    pl.semaphore_wait(barrier, greetings)
    moves_first = exchange(sent_first, came_first, send_first, recv_first)

    got_in.wait()
    place_ids = lax.broadcasted_iota(jnp.int32, (slots, slots), 1)
    for j in range(len(DIRECTIONS)):
        listed = jnp.broadcast_to(in_rows[j].astype(jnp.float32), (slots, slots)).T
        for t in range(head // slots):
            placer[j * slots : (j + 1) * slots, t * slots : (t + 1) * slots] = (
                listed == (place_ids + t * slots).astype(jnp.float32)
            ).astype(jnp.bfloat16)
    got_rhs.wait()
    got_tail.wait()
    residual_tail = row_mask[:, head:] * (rhs[:, head:] - dot(iterate_bf, stiff[:, head:]))
    results[1, :, head:] = residual_tail
    got_basis.wait()
    basis_pad[...] = jnp.zeros_like(basis_pad)
    basis_pad[:vectors, :] = basis[...]
    slot_basis[...] = dot_t(
        placer[...], basis_pad[:, :head] * row_mask[:, :head].astype(jnp.bfloat16)
    ).astype(jnp.bfloat16)
    own_head = row_mask[:, :head] * (rhs[:, :head] - product_head)
    own_residual = jnp.concatenate([own_head, residual_tail], axis=1)
    own_coarse = exact_dot(own_residual, basis_pad[...], dot_t)

    wait_arrivals(moves_first)
    arrived = arrived_slots(came_first)
    gathered[me] = own_coarse - exact_dot(arrived, slot_basis[...])

    def share(slabs, device, send_sem, recv_sem):
        pltpu.make_async_remote_copy(
            src_ref=gathered.at[slabs],
            dst_ref=gathered.at[slabs],
            send_sem=send_sem,
            recv_sem=recv_sem,
            device_id=device,
            device_id_type=MESH,
        ).start()

    def wait_slabs(count, sem):
        some = gathered.at[pl.ds(0, count)]
        pltpu.make_async_copy(some, some, sem).wait()

    for step in team_steps:
        share(pl.ds(me, 1), team_mate(step), team_send, team_recv)

    got_weights.wait()
    scale = weights[...].reshape(1, order_pad) * row_mask
    scaled_basis = scale * basis[...].astype(jnp.float32)
    picked_basis = exact_dot(scaled_basis[:, :head], picker[...])

    got_coarse.wait()
    group = math.lcm(vectors, LANES) // vectors
    lane_ids = lax.broadcasted_iota(jnp.int32, (vectors, LANES), 1)

    def spread(block, carry):
        base = pl.multiple_of(block * group * vectors, LANES)
        tiles = [
            coarse[:, pl.ds(base + t * LANES, LANES)] for t in range(group * vectors // LANES)
        ]
        for r in range(group):
            tile, first = divmod(r * vectors, LANES)
            moved = pltpu.roll(tiles[tile], LANES - first, 1) if first else tiles[tile]
            if first + vectors > LANES:
                following = pltpu.roll(tiles[tile + 1], LANES - first, 1)
                moved = jnp.where(lane_ids < LANES - first, moved, following)
            coarse_pad[block * group + r] = jnp.where(lane_ids < vectors, moved, 0.0)
        return carry

    lax.fori_loop(0, devices // group, spread, 0)

    mates = team * n_sub
    wait_slabs(mates - 1, team_recv)
    for step in column_steps:
        share(pl.ds(team_first * n_sub, mates), column_mate(step), column_send, column_recv)

    residual_head = own_head - row_mask[:, :head] * exact_dot(arrived, placer[...])
    residual_bf = jnp.concatenate([residual_head, residual_tail], axis=1).astype(jnp.bfloat16)
    results[1, :, :head] = residual_head
    got_inverse.wait()
    fixed = scale * dot(residual_bf, inverse[...])
    picked_fix = exact_dot(fixed[:, :head], picker[...])
    base_out = iterate + fixed

    wait_slabs(devices - mates, column_recv)

    def accumulate(block, sums):
        sums = list(sums)
        for r in range(group):
            d = block * group + r
            terms, rows = gathered[d], coarse_pad[d]
            for l in range(loads):
                sums[l] = sums[l] + terms[l : l + 1, :] * rows
        return tuple(sums)

    sums = tuple(jnp.zeros((vectors, LANES), jnp.float32) for _ in range(loads))
    if devices // group <= 4:
        for block in range(devices // group):
            sums = accumulate(block, sums)
    else:
        sums = lax.fori_loop(0, devices // group, accumulate, sums)
    coarse_columns = [
        jnp.sum(s, axis=1, keepdims=True).astype(jnp.bfloat16).astype(jnp.float32) for s in sums
    ]

    def spanned(block):
        return jnp.concatenate(
            [jnp.sum(c * block, axis=0, keepdims=True) for c in coarse_columns], axis=0
        )

    picked = picked_fix + spanned(picked_basis)
    for j in range(len(DIRECTIONS)):
        sent_second[j] = picked[:, j * slots : (j + 1) * slots]
    moves_second = exchange(sent_second, came_second, send_second, recv_second)

    base_out = base_out + spanned(scaled_basis)
    results[0, :, head:] = base_out[:, head:]
    for copy, sends, _ in moves_first + moves_second:
        pl.when(sends)(copy.wait_send)
    wait_slabs(mates - 1, team_send)
    wait_slabs(devices - mates, column_send)
    wait_arrivals(moves_second)
    placed = exact_dot(arrived_slots(came_second), placer[...])
    results[0, :, :head] = base_out[:, :head] + placed


def per_device(
    n_dom,
    n_sub,
    rhs,
    start,
    stiffness,
    local_inverse,
    basis,
    weights,
    coarse_inverse,
    orders,
    out_rows,
    out_counts,
    in_rows,
):
    loads, order_pad = rhs.shape
    directions, slots = out_rows.shape[1:]
    team = max(t for t in range(1, n_dom + 1) if n_dom % t == 0 and (t == 1 or t * t * n_sub <= n_dom))
    vectors = basis.shape[0]
    devices = n_dom * n_sub
    head = -(-(order_pad // 4) // LANES) * LANES
    operands = (
        rhs,
        start,
        stiffness,
        local_inverse,
        basis,
        weights,
        coarse_inverse,
        orders.reshape(1, 1),
        out_rows.transpose(1, 0, 2),
        out_counts,
        in_rows.transpose(1, 0, 2),
    )
    f32 = jnp.float32
    shared = pltpu.VMEM((directions, loads, slots), f32)
    dma = pltpu.SemaphoreType.DMA
    in_hbm = pl.BlockSpec(memory_space=pltpu.HBM)
    both = pltpu.VMEM((2, loads, order_pad), f32)
    results = pl.pallas_call(
        functools.partial(kernel, n_dom, n_sub, team),
        out_shape=both,
        in_specs=[in_hbm] * len(operands),
        out_specs=pl.BlockSpec(memory_space=pltpu.VMEM),
        scratch_shapes=[pltpu.VMEM(x.shape, x.dtype) for x in operands]
        + [
            pltpu.VMEM((head, directions * slots), jnp.bfloat16),
            pltpu.VMEM((directions * slots, head), jnp.bfloat16),
            pltpu.VMEM((LANES, order_pad), jnp.bfloat16),
            pltpu.VMEM((directions * slots, LANES), jnp.bfloat16),
            pltpu.VMEM((devices, vectors, LANES), f32),
            shared,
            shared,
            shared,
            shared,
            pltpu.VMEM((devices, loads, LANES), f32),
            dma((12,)),
            dma((directions,)),
            dma((directions,)),
            dma((directions,)),
            dma((directions,)),
            dma,
            dma,
            dma,
            dma,
        ],
        compiler_params=pltpu.CompilerParams(
            collective_id=0, has_side_effects=True, vmem_limit_bytes=63 * 1024 * 1024
        ),
    )(*operands)
    return results[0], results[1]


def solution(mesh):
    return jax.shard_map(
        functools.partial(per_device, mesh.shape["dom"], mesh.shape["sub"]),
        mesh=mesh,
        in_specs=(
            P(None, ("dom", "sub")),
            P(None, ("dom", "sub")),
            P(("dom", "sub"), None),
            P(("dom", "sub"), None),
            P(None, ("dom", "sub")),
            P(("dom", "sub")),
            P(("dom", "sub"), None),
            P(("dom", "sub")),
            P(("dom", "sub"), None, None),
            P(("dom", "sub"), None),
            P(("dom", "sub"), None, None),
        ),
        out_specs=(P(None, ("dom", "sub")), P(None, ("dom", "sub"))),
        check_vma=False,
    )
```
